256 devices in a mesh: aux: 32 (over x, z), occ: 8 (over y, core).
Axes of the slice: x: 4, y: 4, z: 8, core: 2. Of those that a mesh axis runs over, the one named last changes fastest.
Arguments:
- blocks: float32 [1536, 16, 4096], P('aux', 'occ'), may hold values from -6 to 6
- pair_list: int32 [32, 16, 2], P('aux', 'occ'), may hold values from 0 to 15
- pair_count: int32 [32], P('aux'), may hold values from 4 to 16, as said below
- orbitals: float32 [128, 1024], replicated, may hold values from -0.0009765625 to 0.0009765625
Outputs:
- exchange: float32 [1024, 1024], P('aux', 'occ')
The draws below stay inside these ranges and needn't reach their ends.
Inputs may be any that keep to these rules, and one draw needn't show every extreme that they name: `pair_list`: block indices of the kept pairs; pairs may repeat. `pair_count`: slots at or beyond an auxiliary block's count are padding and contribute nothing; some auxiliary block uses all 16 slots.
All inputs are finite; a program needn't handle non-finite values.
Results may differ from the reference program's by a relative error of at most 0.0003.
Values sent between devices are 32-bit elements; how exact they have to be, the bound alone decides.
No kernel may reach another device: no remote copies, remote signals or barrier semaphores. Data moves between devices by JAX's collectives and lax.ppermute only.
A program may use at most 64 MiB of HBM per device.

```python
import jax
import jax.numpy as jnp
from jax import lax

NBF = 1024
BLK = 64
NOCC = 128
AUX_DEV = 48
NB = 16
KEPT = 16
NAUX = 1536
N_AUX = 32


def draw_pair_count(key, part):
    counts = jax.random.randint(key, (N_AUX,), KEPT // 4, KEPT + 1).astype(jnp.int32)
    position = jax.random.randint(jax.random.fold_in(key, 7), (), 0, N_AUX)
    return counts.at[position].set(KEPT).astype(jnp.int32)


def place_ends(drawn, own_key, smallest, high):
    longest = drawn.shape.index(max(drawn.shape))
    spots = []
    for shift in (0, 1):
        where = [jax.random.randint(jax.random.fold_in(own_key, axis), (), 0, length) for axis, length in enumerate(drawn.shape)]
        where[longest] = (where[longest] + shift) % drawn.shape[longest]
        spots.append(tuple(where))
    return drawn.at[spots[0]].set(smallest).at[spots[1]].set(high)


def block_scale(key, shape, pieces, least, high):
    loudness, own = 1.0, jax.random.fold_in(key, 6)
    for dim, blocks in pieces:
        steps = jnp.exp(jax.random.uniform(jax.random.fold_in(own, dim), (blocks,), jnp.float32, least / len(pieces), high / len(pieces)))
        loudness = loudness * jnp.repeat(steps, shape[dim] // blocks).reshape([-1 if axis == dim else 1 for axis in range(len(shape))])
    return loudness


def scatter_about(key, dims, deviation, limit, pieces=(), kind=jnp.bfloat16):
    entries = deviation * jax.random.normal(key, dims, jnp.float32)
    if pieces:
        entries = entries * block_scale(key, dims, pieces, -0.22, 0.18)
    return jnp.clip(entries, -limit, limit).astype(kind)


def setup_inputs(seed: int = 0) -> dict:
    key_of = jax.random.split(jax.random.key(seed), 5)
    blocks = scatter_about(key_of[0], (NAUX, KEPT, BLK * BLK), 1.0, 6.0, ((0, 32), (1, 8)), jnp.float32)
    pair_list = place_ends(jax.random.randint(key_of[1], (N_AUX, KEPT, 2), 0, NB), jax.random.fold_in(key_of[1], 1), 0, NB - 1).astype(jnp.int32)
    pair_count = draw_pair_count(jax.random.fold_in(key_of[4], 71), 0)
    orbitals = scatter_about(key_of[3], (NOCC, NBF), (160 * AUX_DEV * N_AUX * NOCC) ** -0.5, 0.0009765625, (), jnp.float32)
    return {"blocks": blocks, "pair_list": pair_list, "pair_count": pair_count, "orbitals": orbitals}


def reference(blocks, pair_list, pair_count, orbitals):
    n_blocks = NBF // BLK
    coefficients = orbitals.reshape(NOCC, n_blocks, BLK)
    tile_data = blocks.reshape(N_AUX, AUX_DEV, KEPT, BLK, BLK)
    positions = jnp.arange(n_blocks, dtype=jnp.int32)
    slot_index = jnp.arange(KEPT, dtype=jnp.int32)

    def one_block(total, inputs):
        tiles_here, pairs_here, count_here = inputs
        live_slot = slot_index < count_here
        row_onehot = ((pairs_here[:, 0][:, None] == positions[None, :]) & live_slot[:, None]).astype(jnp.float32)
        col_onehot = (pairs_here[:, 1][:, None] == positions[None, :]).astype(jnp.float32)
        picked_cols = jnp.einsum('iNn,sN->sin', coefficients, col_onehot, precision=lax.Precision.HIGHEST)
        half_tiles = jnp.einsum('qsmn,sin->isqm', tiles_here, picked_cols, precision=lax.Precision.HIGHEST)
        transformed = jnp.einsum('isqm,sM->iqMm', half_tiles, row_onehot, precision=lax.Precision.HIGHEST)
        transformed = transformed.reshape(NOCC * AUX_DEV, NBF)
        partial_value = jnp.einsum('rm,rn->mn', transformed, transformed, precision=lax.Precision.HIGHEST)
        return total + partial_value, None

    total, _ = lax.scan(one_block, jnp.zeros((NBF, NBF), jnp.float32), (tile_data, pair_list, pair_count))
    return total
```

```python
import functools

import jax
import jax.numpy as jnp
from jax import lax
from jax.experimental import pallas as pl
from jax.experimental.layout import Layout, with_layout_constraint
from jax.experimental.pallas import tpu as pltpu
from jax.sharding import PartitionSpec as P

NBF = 1024
BLK = 64
NOCC = 128
AUX_DEV = 48
NX, NZ, NY, NC = 4, 8, 4, 2
CHUNKS = (8, 4)
ROWS = BLK // 2
HEAD = 8
VMEM = pl.BlockSpec(memory_space=pltpu.VMEM)
SMEM = pl.BlockSpec(memory_space=pltpu.SMEM)
F32, BF16 = jnp.float32, jnp.bfloat16
NT = (((1,), (1,)), ((), ()))


def device_of(x, z, y, c):
    return ((x % NX) * NZ + z % NZ) * (NY * NC) + (y % NY) * NC + c % NC


def send(array, where):
    pairs = [
        (device_of(x, z, y, c), device_of(*where(x, z, y, c)))
        for x in range(NX)
        for z in range(NZ)
        for y in range(NY)
        for c in range(NC)
    ]
    return lax.ppermute(array, ("aux", "occ"), pairs)


def call(kernel, out_shape, in_specs, scratch=(), flops=0, bytes_accessed=0):
    return pl.pallas_call(
        kernel,
        out_shape=out_shape,
        in_specs=in_specs,
        out_specs=jax.tree.map(lambda _: VMEM, out_shape),
        scratch_shapes=list(scratch),
        compiler_params=pltpu.CompilerParams(vmem_limit_bytes=40 * 2**20),
        cost_estimate=pl.CostEstimate(
            flops=flops, bytes_accessed=bytes_accessed, transcendentals=0
        ),
    )


def split(values):
    high = values.astype(BF16)
    return high, (values - high.astype(F32)).astype(BF16)


def pack_kernel(info_ref, tiles_ref, *outs):
    lane = lax.broadcasted_iota(jnp.int32, (HEAD, 128), 1)
    head = jnp.zeros((HEAD, 128), F32)
    for j in range(6):
        head = jnp.where(lane == j, info_ref[1 + j].astype(F32), head)
    start = 0
    for chunk, count in enumerate(CHUNKS):
        for step in range(NY):
            out = outs[chunk * NY + step]
            chip = lax.rem(info_ref[0] + step, NY)
            base = (chip * (AUX_DEV // NY) + start) * BLK
            for slot in range(2):
                out[pl.ds(slot * count * ROWS, count * ROWS), :] = tiles_ref[
                    pl.ds(pl.multiple_of(base, 8) + slot, count * ROWS, stride=2), :
                ]
            if chunk == 0:
                out[pl.ds(2 * count * ROWS, HEAD), :] = head
        start += count


def weights_kernel(info_ref, orbitals_ref, both_ref, low_ref, high_t, low_t):
    high, low = split(orbitals_ref[...].T)
    high_t[...] = high
    low_t[...] = low
    zero = jnp.zeros((BLK, NOCC), BF16)
    for slot in range(16):
        column = pl.multiple_of(info_ref[slot, 1] * BLK, BLK)
        live = info_ref[slot, 2] > 0
        high = jnp.where(live, high_t[pl.ds(column, BLK), :].astype(F32), 0.0).astype(BF16)
        low = jnp.where(live, low_t[pl.ds(column, BLK), :].astype(F32), 0.0).astype(BF16)
        for half in range(2):
            both_ref[slot, pl.ds(half * 128, BLK), 0:128] = high
            both_ref[slot, pl.ds(half * 128, BLK), 128:256] = zero
            both_ref[slot, pl.ds(half * 128 + BLK, BLK), 0:128] = zero
            both_ref[slot, pl.ds(half * 128 + BLK, BLK), 128:256] = high
        low_ref[slot, 0:BLK, 0:128] = low
        low_ref[slot, 0:BLK, 128:256] = zero
        low_ref[slot, BLK:128, 0:128] = zero
        low_ref[slot, BLK:128, 128:256] = low


def product_kernel(count, first, last, info_ref, place_ref, both_ref, low_ref, *refs):
    payloads = refs[:8]
    refs = refs[8:]
    if not first:
        before, refs = refs[0], refs[1:]
    if last:
        outs, refs = refs[:4], refs[4:]
    else:
        outs, refs = refs[:1], refs[1:]
    half, high_ref, low_half_ref, total = refs
    y, x, core = place_ref[0], place_ref[1], place_ref[2]
    half[...] = jnp.zeros_like(half)
    for source in range(8):
        for slot in range(2):
            index = source * 2 + slot
            tiles = payloads[source][pl.ds(slot * count * ROWS, count * ROWS), :]
            high, low = split(tiles)
            part = jnp.dot(
                jnp.concatenate([high, low], axis=1), both_ref[index], preferred_element_type=F32
            ) + jnp.dot(high, low_ref[index], preferred_element_type=F32)
            row = pl.multiple_of(info_ref[index, 0] * BLK, BLK)
            for q in range(count):
                for odd in range(2):
                    spot = pl.ds(row + odd, ROWS, stride=2)
                    half[q, spot, :] += part[q * ROWS : (q + 1) * ROWS, odd * 128 : odd * 128 + 128]
    for q in range(count):
        high, low = split(half[q])
        high_ref[:, q * 128 : (q + 1) * 128] = high
        low_half_ref[:, q * 128 : (q + 1) * 128] = low

    def columns(ref, step):
        start = (lax.rem(y + step, NY) * NC + core) * 128
        return ref[pl.ds(pl.multiple_of(start, 128), 128), :]

    for pair in range(2):
        col_high = jnp.concatenate([columns(high_ref, 2 * pair + j) for j in range(2)], axis=0)
        col_low = jnp.concatenate([columns(low_half_ref, 2 * pair + j) for j in range(2)], axis=0)
        where = slice(pair * 256, pair * 256 + 256)
        value = lax.dot_general(high_ref[...], col_high, NT, preferred_element_type=F32)
        value += lax.dot_general(high_ref[...], col_low, NT, preferred_element_type=F32)
        value += lax.dot_general(low_half_ref[...], col_high, NT, preferred_element_type=F32)
        if not first:
            value += before[:, where]
        if last:
            total[:, where] = value
        else:
            outs[0][:, where] = value
    if last:
        for which in range(2):

            @pl.when(core == which)
            def _():
                for a in range(4):
                    for b in range(4):
                        i, j = (b, a) if which == 0 else (a, b)
                        start = pl.multiple_of(lax.rem(x + i, NX) * 256, 256)
                        outs[a][b] = total[pl.ds(start, 256), j * 128 : (j + 1) * 128]


def per_device(blocks, pair_list, pair_count, orbitals):
    aux, occ = lax.axis_index("aux"), lax.axis_index("occ")
    x, y, core = aux // NZ, occ // NC, occ % NC
    live = (2 * occ + jnp.arange(2) < pair_count[0]).astype(jnp.int32)
    own = jnp.concatenate([pair_list[0], live[:, None]], axis=1).reshape(6)
    info = jnp.concatenate([y[None], own]).astype(jnp.int32)
    place = jnp.stack([y, x, core]).astype(jnp.int32)
    tiles = blocks.reshape(AUX_DEV, 2, ROWS, 128)
    tiles = with_layout_constraint(tiles, Layout(major_to_minor=(0, 2, 1, 3)))
    tiles = tiles.transpose(0, 2, 1, 3).reshape(AUX_DEV * BLK, 128)

    def payload(chunk):
        return jax.ShapeDtypeStruct(
            (2 * CHUNKS[chunk] * ROWS + (HEAD if chunk == 0 else 0), 128), F32
        )

    packed = call(pack_kernel, [payload(c) for c in range(2) for _ in range(NY)], [SMEM, VMEM])(
        info, tiles
    )
    arrived = []
    for chunk in range(2):
        mine = packed[chunk * NY : chunk * NY + NY]
        got = [mine[0]] + [
            send(mine[k], lambda x, z, y, c, k=k: (x, z, y + k, c)) for k in (2, 1, 3)
        ]
        other = [send(part, lambda x, z, y, c: (x, z, y, c + 1)) for part in got]
        arrived.append(got + other)
    heads = jnp.stack([part[2 * CHUNKS[0] * ROWS, :6] for part in arrived[0]])
    pairs = heads.astype(jnp.int32).reshape(16, 3)
    both, low = call(
        weights_kernel,
        [jax.ShapeDtypeStruct((16, 256, 256), BF16), jax.ShapeDtypeStruct((16, 128, 256), BF16)],
        [SMEM, VMEM],
        [pltpu.VMEM((NBF, NOCC), BF16)] * 2,
    )(pairs, orbitals)
    total = None
    for chunk, count in enumerate(CHUNKS):
        first, last = chunk == 0, chunk == 1
        outs = (
            [jax.ShapeDtypeStruct((4, 256, 128), F32)] * 4
            if last
            else [jax.ShapeDtypeStruct((NBF, 512), F32)]
        )
        total = call(
            functools.partial(product_kernel, count, first, last),
            outs,
            [SMEM, SMEM] + [VMEM] * (10 if first else 11),
            [
                pltpu.VMEM((count, NBF, NOCC), F32),
                pltpu.VMEM((NBF, count * NOCC), BF16),
                pltpu.VMEM((NBF, count * NOCC), BF16),
                pltpu.VMEM((NBF, 512) if last else (8, 128), F32),
            ],
            flops=2 * 3 * NBF * 512 * count * NOCC,
        )(pairs, place, both, low, *arrived[chunk], *([] if first else total))

    def along(k, swapped):
        def where(x, z, y, c):
            return (x + k, z, y, c) if (c == 1) != swapped else (x, z, y + k, c)

        return where

    summed = total[0]
    got = [send(total[k], along(k, False)) for k in (2, 1, 3)]
    summed = total[0] + got[0] + got[1] + got[2]
    got = [send(summed[k], along(k, True)) for k in (2, 1, 3)]
    summed = summed[0] + got[0] + got[1] + got[2]
    groups = [[a * NZ + b for b in range(NZ)] for a in range(NX)]
    parts = lax.all_to_all(
        summed.reshape(NZ, 32, 128), "aux", 0, 0, axis_index_groups=groups, tiled=True
    )
    return jnp.sum(parts, axis=0)


def solution(mesh):
    in_specs = (P("aux", "occ", None), P("aux", "occ", None), P("aux"), P())
    return jax.shard_map(
        per_device, mesh=mesh, in_specs=in_specs, out_specs=P("aux", "occ"), check_vma=False
    )
```

```python
import functools

import jax
import jax.numpy as jnp
from jax import lax
from jax.experimental import pallas as pl
from jax.experimental.layout import Layout, with_layout_constraint
from jax.experimental.pallas import tpu as pltpu
from jax.sharding import PartitionSpec as P

NBF = 1024
BLK = 64
NOCC = 128
AUX_DEV = 48
NX, NZ, NY, NC = 4, 8, 4, 2
CHIP_AUX = AUX_DEV // NY
CHUNKS = (8, 4)
STEPS = (2, 1, 3)
ROWS = BLK // 2
HEAD = 8
ORDER = 10**11
PAD = 8
VMEM = pl.BlockSpec(memory_space=pltpu.VMEM)
SMEM = pl.BlockSpec(memory_space=pltpu.SMEM)
F32, BF16 = jnp.float32, jnp.bfloat16
NT = (((1,), (1,)), ((), ()))


def device_of(x, z, y, c):
    return ((x % NX) * NZ + z % NZ) * (NY * NC) + (y % NY) * NC + c % NC


def send(array, where):
    pairs = [
        (device_of(x, z, y, c), device_of(*where(x, z, y, c)))
        for x in range(NX)
        for z in range(NZ)
        for y in range(NY)
        for c in range(NC)
    ]
    return lax.ppermute(array, ("aux", "occ"), pairs)


def call(kernel, out_shape, in_specs, scratch=(), flops=0, bytes_accessed=0):
    return pl.pallas_call(
        kernel,
        out_shape=out_shape,
        in_specs=in_specs,
        out_specs=jax.tree.map(lambda _: VMEM, out_shape),
        scratch_shapes=list(scratch),
        compiler_params=pltpu.CompilerParams(vmem_limit_bytes=40 * 2**20),
        cost_estimate=pl.CostEstimate(
            flops=flops, bytes_accessed=bytes_accessed, transcendentals=0
        ),
    )


def split(values):
    high = values.astype(BF16)
    return high, (values - high.astype(F32)).astype(BF16)


def pack_kernel(pairs_ref, count_ref, tiles_ref, own, *outs):
    occ = lax.axis_index("occ")
    lane = lax.broadcasted_iota(jnp.int32, (HEAD, 128), 1)
    head = jnp.zeros((HEAD, 128), F32)
    for slot in range(2):
        live = (occ * 2 + slot < count_ref[0]).astype(jnp.int32)
        for j, number in enumerate((pairs_ref[0, slot, 0], pairs_ref[0, slot, 1], live)):
            head = jnp.where(lane == 3 * slot + j, number.astype(F32), head)

    def fill(out, step, start, count, headed):
        chip = lax.rem(occ // NC + step, NY)
        base = (chip * CHIP_AUX + start) * BLK
        for slot in range(2):
            out[pl.ds(slot * count * ROWS, count * ROWS), :] = tiles_ref[
                pl.ds(pl.multiple_of(base, 8) + slot, count * ROWS, stride=2), :
            ]
        if headed:
            out[pl.ds(2 * count * ROWS, HEAD), :] = head

    fill(own, 0, 0, CHIP_AUX, True)
    for j, step in enumerate(STEPS):
        fill(outs[j], step, 0, CHUNKS[0], True)
        fill(outs[3 + j], step, CHUNKS[0], CHUNKS[1], False)


def orbitals_kernel(orbitals_ref, high_ref, low_ref):
    high, low = split(orbitals_ref[...].T)
    high_ref[...] = high
    low_ref[...] = low


def picked(ref, info_ref, index):
    column = pl.multiple_of(info_ref[index, 1] * BLK, BLK)
    block = ref[pl.ds(column, BLK), :].astype(F32)
    block = jnp.where(info_ref[index, 2] > 0, block, 0.0).astype(BF16)
    zero = jnp.zeros((BLK, NOCC), BF16)
    top = jnp.concatenate([block, zero], axis=1)
    return jnp.concatenate([top, jnp.concatenate([zero, block], axis=1)], axis=0)


def half_kernel(chunk, info_ref, high_t, low_t, own, own_other, *refs):
    got, (got_other, high_ref, low_ref, half, parts) = refs[:3], refs[3:]
    count, head = CHUNKS[chunk], HEAD if chunk == 0 else 0
    sources = [(ref, CHIP_AUX * ROWS, chunk * CHUNKS[0] * ROWS) for ref in (own, own_other)]
    sources += [(ref, count * ROWS, 0) for ref in got]
    sources += [(got_other, count * ROWS, j * (2 * count * ROWS + head)) for j in range(3)]
    half[...] = jnp.zeros_like(half)
    for source, (ref, stride, start) in enumerate(sources):
        for slot in range(2):
            index = source * 2 + slot
            high, low = split(ref[pl.ds(start + slot * stride, count * ROWS), :])
            weights = picked(high_t, info_ref, index)
            parts[index] = jnp.dot(
                jnp.concatenate([high, low], axis=1),
                jnp.concatenate([weights, weights], axis=0),
                preferred_element_type=F32,
            ) + jnp.dot(high, picked(low_t, info_ref, index), preferred_element_type=F32)
    for index in range(16):
        row = pl.multiple_of(info_ref[index, 0] * BLK, BLK)
        for q in range(count):
            for odd in range(2):
                spot = pl.ds(row + odd, ROWS, stride=2)
                half[q, spot, :] += parts[
                    index, q * ROWS : (q + 1) * ROWS, odd * 128 : odd * 128 + 128
                ]
    for q in range(count):
        high, low = split(half[q])
        high_ref[:, q * 128 : (q + 1) * 128] = high
        low_ref[:, q * 128 : (q + 1) * 128] = low


def exchange_kernel(steps, *refs):
    halves, outs = refs[:4], refs[4:]
    aux, occ = lax.axis_index("aux"), lax.axis_index("occ")
    x, y, core = aux // NZ, occ // NC, lax.rem(occ, NC)

    def rows(ref, i):
        return ref[pl.ds(pl.multiple_of(lax.rem(x + i, NX) * 256, 256), 256), :]

    def columns(ref, j):
        start = (lax.rem(y + j, NY) * NC + core) * 128
        return ref[pl.ds(pl.multiple_of(start, 128), 128), :]

    def product(row_steps, column_steps):
        value = None
        for part in range(2):
            high_ref, low_ref = halves[2 * part], halves[2 * part + 1]
            high, low = (
                jnp.concatenate([rows(ref, i) for i in row_steps], axis=0)
                for ref in (high_ref, low_ref)
            )
            col_high, col_low = (
                jnp.concatenate([columns(ref, j) for j in column_steps], axis=0)
                for ref in (high_ref, low_ref)
            )
            for left, right in ((high, col_high), (high, col_low), (low, col_high)):
                term = lax.dot_general(left, right, NT, preferred_element_type=F32)
                value = term if value is None else value + term
        return value

    @pl.when(core == 0)
    def _():
        value = product(range(NX), steps)
        for a in range(2):
            for b in range(4):
                outs[a][b * 256 : (b + 1) * 256] = value[b * 256 : (b + 1) * 256, a * 128 : (a + 1) * 128]

    @pl.when(core == 1)
    def _():
        for pair in range(2):
            value = product(steps, (2 * pair, 2 * pair + 1))
            for a in range(2):
                for b in range(2):
                    outs[a][(2 * pair + b) * 256 : (2 * pair + b + 1) * 256] = value[
                        a * 256 : (a + 1) * 256, b * 128 : (b + 1) * 128
                    ]
    for out in outs:
        if out.shape[0] > 1024:
            out[1024:] = jnp.zeros((out.shape[0] - 1024, 128), F32)


def per_device(blocks, pair_list, pair_count, orbitals):
    shape = jax.ShapeDtypeStruct
    tiles = blocks.reshape(AUX_DEV, 2, ROWS, 128)
    tiles = with_layout_constraint(tiles, Layout(major_to_minor=(0, 2, 1, 3)))
    tiles = tiles.transpose(0, 2, 1, 3).reshape(AUX_DEV * BLK, 128)
    first, second = CHUNKS
    own, *packed = call(
        pack_kernel,
        [shape((2 * CHIP_AUX * ROWS + HEAD, 128), F32)]
        + [shape((2 * first * ROWS + HEAD, 128), F32)] * 3
        + [shape((2 * second * ROWS, 128), F32)] * 3,
        [SMEM, SMEM, VMEM],
    )(pair_list, pair_count, tiles)
    high_t, low_t = call(orbitals_kernel, [shape((NBF, NOCC), BF16)] * 2, [VMEM], flops=ORDER)(orbitals)

    def over_y(mine):
        return [
            send(part, lambda x, z, y, c, k=k: (x, z, y + k, c))
            for part, k in zip(mine, STEPS, strict=True)
        ]

    def over_core(part):
        return send(part, lambda x, z, y, c: (x, z, y, c + 1))

    later = over_y(packed[3:])
    got = over_y(packed[:3])
    own_other = over_core(own)
    got_other = over_core(jnp.concatenate(got))
    size = 2 * first * ROWS + HEAD
    heads = [own[2 * CHIP_AUX * ROWS], own_other[2 * CHIP_AUX * ROWS]]
    heads += [part[size - HEAD] for part in got]
    heads += [got_other[(j + 1) * size - HEAD] for j in range(3)]
    pairs = jnp.stack(heads)[:, :6].astype(jnp.int32).reshape(16, 3)

    def half(chunk, *parts):
        count = CHUNKS[chunk]
        return call(
            functools.partial(half_kernel, chunk),
            [shape((NBF, count * NOCC), BF16)] * 2,
            [SMEM] + [VMEM] * 8,
            [pltpu.VMEM((count, NBF, NOCC), F32), pltpu.VMEM((16, count * ROWS, 256), F32)],
        )(pairs, high_t, low_t, own, own_other, *parts)

    halves = list(half(0, *got, got_other))
    halves[0], *later = lax.optimization_barrier((halves[0], *later))
    halves += half(1, *later, over_core(jnp.concatenate(later)))

    def along(k, swapped):
        def where(x, z, y, c):
            return (x + k, z, y, c) if (c == 1) != swapped else (x, z, y + k, c)

        return where

    def partial(steps):
        return call(
            functools.partial(exchange_kernel, steps),
            [shape((4 * 256 + (0 if 0 in steps else PAD), 128), F32)] * 2,
            [VMEM] * 4,
            flops=2 * 3 * 256 * 1024 * CHIP_AUX * NOCC,
        )(*halves)

    two, one = partial((2, 1))
    three, summed = partial((3, 0))
    for part, k in ((two, 2), (one, 1), (three, 3)):
        summed += send(part, along(k, False))[:1024]
    summed = summed.reshape(4, 256, 128)
    got = [send(summed[k], along(k, True)) for k in STEPS]
    summed = summed[0] + got[0] + got[1] + got[2]
    groups = [[a * NZ + b for b in range(NZ)] for a in range(NX)]
    parts = lax.all_to_all(
        summed.reshape(NZ, 32, 128), "aux", 0, 0, axis_index_groups=groups, tiled=True
    )
    return jnp.sum(parts, axis=0)


def solution(mesh):
    in_specs = (P("aux", "occ", None), P("aux", "occ", None), P("aux"), P())
    return jax.shard_map(
        per_device, mesh=mesh, in_specs=in_specs, out_specs=P("aux", "occ"), check_vma=False
    )
```

```python
import functools

import jax
import jax.numpy as jnp
from jax import lax
from jax.experimental import pallas as pl
from jax.experimental.layout import Layout, with_layout_constraint
from jax.experimental.pallas import tpu as pltpu
from jax.sharding import PartitionSpec as P

NBF = 1024
BLK = 64
NOCC = 128
AUX_DEV = 48
NX, NZ, NY, NC = 4, 8, 4, 2
CHIP_AUX = AUX_DEV // NY
CHUNKS = (6, 6)
STEPS = (2, 1, 3)
ROWS = BLK // 2
HEAD = 8
ORDER = 10**11
PAD = 8
VMEM = pl.BlockSpec(memory_space=pltpu.VMEM)
SMEM = pl.BlockSpec(memory_space=pltpu.SMEM)
F32, BF16 = jnp.float32, jnp.bfloat16
NT = (((1,), (1,)), ((), ()))


def device_of(x, z, y, c):
    return ((x % NX) * NZ + z % NZ) * (NY * NC) + (y % NY) * NC + c % NC


def send(array, where):
    pairs = [
        (device_of(x, z, y, c), device_of(*where(x, z, y, c)))
        for x in range(NX)
        for z in range(NZ)
        for y in range(NY)
        for c in range(NC)
    ]
    return lax.ppermute(array, ("aux", "occ"), pairs)


def call(kernel, out_shape, in_specs, scratch=(), flops=0, bytes_accessed=0):
    return pl.pallas_call(
        kernel,
        out_shape=out_shape,
        in_specs=in_specs,
        out_specs=jax.tree.map(lambda _: VMEM, out_shape),
        scratch_shapes=list(scratch),
        compiler_params=pltpu.CompilerParams(vmem_limit_bytes=40 * 2**20),
        cost_estimate=pl.CostEstimate(
            flops=flops, bytes_accessed=bytes_accessed, transcendentals=0
        ),
    )


def split(values):
    high = values.astype(BF16)
    return high, (values - high.astype(F32)).astype(BF16)


def pack_kernel(pairs_ref, count_ref, tiles_ref, own, *outs):
    occ = lax.axis_index("occ")
    lane = lax.broadcasted_iota(jnp.int32, (HEAD, 128), 1)
    head = jnp.zeros((HEAD, 128), F32)
    for slot in range(2):
        live = (occ * 2 + slot < count_ref[0]).astype(jnp.int32).astype(F32)
        head = jnp.where(lane == 3 * slot + 2, live, head)
        for j in range(2):
            number = pairs_ref[0, slot : slot + 1, j : j + 1].astype(F32)
            head = jnp.where(lane == 3 * slot + j, jnp.broadcast_to(number, head.shape), head)

    def fill(out, step, start, count, headed):
        chip = lax.rem(occ // NC + step, NY)
        base = (chip * CHIP_AUX + start) * BLK
        for slot in range(2):
            out[pl.ds(slot * count * ROWS, count * ROWS), :] = tiles_ref[
                pl.ds(pl.multiple_of(base, 8) + slot, count * ROWS, stride=2), :
            ]
        if headed:
            out[pl.ds(2 * count * ROWS, HEAD), :] = head

    fill(own, 0, 0, CHIP_AUX, True)
    for j, step in enumerate(STEPS):
        fill(outs[j], step, 0, CHUNKS[0], True)
        fill(outs[3 + j], step, CHUNKS[0], CHUNKS[1], False)


def orbitals_kernel(orbitals_ref, high_ref, low_ref):
    high, low = split(orbitals_ref[...].T)
    high_ref[...] = high
    low_ref[...] = low


def picked(ref, info_ref, index):
    column = pl.multiple_of(info_ref[index, 1] * BLK, BLK)
    block = ref[pl.ds(column, BLK), :].astype(F32)
    block = jnp.where(info_ref[index, 2] > 0, block, 0.0).astype(BF16)
    zero = jnp.zeros((BLK, NOCC), BF16)
    top = jnp.concatenate([block, zero], axis=1)
    return jnp.concatenate([top, jnp.concatenate([zero, block], axis=1)], axis=0)


def half_kernel(chunk, info_ref, high_t, low_t, own, own_other, *refs):
    got, refs = refs[:3], refs[3:]
    got_other, (high_ref, low_ref, half, parts) = refs[:-4], refs[-4:]
    count, head = CHUNKS[chunk], HEAD if chunk == 0 else 0
    sources = [(ref, CHIP_AUX * ROWS, chunk * CHUNKS[0] * ROWS) for ref in (own, own_other)]
    sources += [(ref, count * ROWS, 0) for ref in got]
    if chunk == 0:
        sources += [(got_other[0], count * ROWS, j * (2 * count * ROWS + head)) for j in range(3)]
    else:
        sources += [(ref, count * ROWS, 0) for ref in got_other]
    half[...] = jnp.zeros_like(half)
    for source, (ref, stride, start) in enumerate(sources):
        for slot in range(2):
            index = source * 2 + slot
            high, low = split(ref[pl.ds(start + slot * stride, count * ROWS), :])
            weights, rest = (picked(ref, info_ref, index) for ref in (high_t, low_t))
            parts[index] = jnp.dot(
                jnp.concatenate([high, low, high], axis=1),
                jnp.concatenate([weights, weights, rest], axis=0),
                preferred_element_type=F32,
            )
    for index in range(16):
        row = pl.multiple_of(info_ref[index, 0] * BLK, BLK)
        for q in range(count):
            for odd in range(2):
                spot = pl.ds(row + odd, ROWS, stride=2)
                half[q, spot, :] += parts[
                    index, q * ROWS : (q + 1) * ROWS, odd * 128 : odd * 128 + 128
                ]
    for q in range(count):
        high, low = split(half[q])
        high_ref[:, q * 128 : (q + 1) * 128] = high
        low_ref[:, q * 128 : (q + 1) * 128] = low


def exchange_kernel(steps, parts, *refs):
    halves, before, outs = refs[: 2 * parts], refs[2 * parts : -2], refs[-2:]
    aux, occ = lax.axis_index("aux"), lax.axis_index("occ")
    x, y, core = aux // NZ, occ // NC, lax.rem(occ, NC)

    def rows(ref, i):
        return ref[pl.ds(pl.multiple_of(lax.rem(x + i, NX) * 256, 256), 256), :]

    def columns(ref, j):
        start = (lax.rem(y + j, NY) * NC + core) * 128
        return ref[pl.ds(pl.multiple_of(start, 128), 128), :]

    def product(row_steps, column_steps):
        high, low = (
            [jnp.concatenate([rows(ref, i) for i in row_steps], axis=0) for ref in halves[n::2]]
            for n in range(2)
        )
        col_high, col_low = (
            [jnp.concatenate([columns(ref, j) for j in column_steps], axis=0) for ref in halves[n::2]]
            for n in range(2)
        )
        return lax.dot_general(
            jnp.concatenate([*high, *high, *low], axis=1),
            jnp.concatenate([*col_high, *col_low, *col_high], axis=1),
            NT,
            preferred_element_type=F32,
        )

    def put(a, b, tile):
        spot = slice(b * 256, b * 256 + 256)
        outs[a][spot] = before[a][spot] + tile if before else tile

    @pl.when(core == 0)
    def _():
        value = product(range(NX), steps)
        for a in range(2):
            for b in range(4):
                put(a, b, value[b * 256 : (b + 1) * 256, a * 128 : (a + 1) * 128])

    @pl.when(core == 1)
    def _():
        for pair in range(2):
            value = product(steps, (2 * pair, 2 * pair + 1))
            for a in range(2):
                for b in range(2):
                    put(
                        a,
                        2 * pair + b,
                        value[a * 256 : (a + 1) * 256, b * 128 : (b + 1) * 128],
                    )

    for out in outs:
        if out.shape[0] > 1024:
            out[1024:] = jnp.zeros((out.shape[0] - 1024, 128), F32)


def per_device(blocks, pair_list, pair_count, orbitals):
    shape = jax.ShapeDtypeStruct
    tiles = blocks.reshape(AUX_DEV, 2, ROWS, 128)
    tiles = with_layout_constraint(tiles, Layout(major_to_minor=(0, 2, 1, 3)))
    tiles = tiles.transpose(0, 2, 1, 3).reshape(AUX_DEV * BLK, 128)
    first, second = CHUNKS
    own, *packed = call(
        pack_kernel,
        [shape((2 * CHIP_AUX * ROWS + HEAD, 128), F32)]
        + [shape((2 * first * ROWS + HEAD, 128), F32)] * 3
        + [shape((2 * second * ROWS, 128), F32)] * 3,
        [VMEM, SMEM, VMEM],
    )(pair_list, pair_count, tiles)
    high_t, low_t = call(orbitals_kernel, [shape((NBF, NOCC), BF16)] * 2, [VMEM], flops=ORDER)(orbitals)

    def over_y(mine):
        return [
            send(part, lambda x, z, y, c, k=k: (x, z, y + k, c))
            for part, k in zip(mine, STEPS, strict=True)
        ]

    def over_core(part):
        return send(part, lambda x, z, y, c: (x, z, y, c + 1))

    later = over_y(packed[3:])
    got = over_y(packed[:3])
    own_other = over_core(own)
    got_other = over_core(jnp.concatenate(got))
    size = 2 * first * ROWS + HEAD
    heads = [own[2 * CHIP_AUX * ROWS], own_other[2 * CHIP_AUX * ROWS]]
    heads += [part[size - HEAD] for part in got]
    heads += [got_other[(j + 1) * size - HEAD] for j in range(3)]
    pairs = jnp.stack(heads)[:, :6].astype(jnp.int32).reshape(16, 3)

    def half(chunk, *parts):
        count = CHUNKS[chunk]
        return call(
            functools.partial(half_kernel, chunk),
            [shape((NBF, count * NOCC), BF16)] * 2,
            [SMEM] + [VMEM] * (4 + len(parts)),
            [pltpu.VMEM((count, NBF, NOCC), F32), pltpu.VMEM((16, count * ROWS, 256), F32)],
        )(pairs, high_t, low_t, own, own_other, *parts)

    def partial(steps, halves, before=()):
        return call(
            functools.partial(exchange_kernel, steps, len(halves) // 2),
            [shape((4 * 256 + (0 if 0 in steps else PAD), 128), F32)] * 2,
            [VMEM] * (len(halves) + len(before)),
            flops=2 * 3 * 256 * 1024 * CHIP_AUX * NOCC,
        )(*halves, *before)

    halves = list(half(0, *got, got_other))
    halves[0], *later = lax.optimization_barrier((halves[0], *later))
    before = partial((1, 3), halves)
    last = half(1, *later, *(over_core(part) for part in later))
    one, three = partial((1, 3), last, before)
    two, summed = partial((2, 0), [*halves, *last])

    def along(k, swapped):
        def where(x, z, y, c):
            return (x + k, z, y, c) if (c == 1) != swapped else (x, z, y + k, c)

        return where

    for part, k in ((one, 1), (three, 3), (two, 2)):
        summed += send(part, along(k, False))[:1024]
    summed = summed.reshape(4, 256, 128)
    got = [send(summed[k], along(k, True)) for k in STEPS]
    summed = summed[0] + got[0] + got[1] + got[2]
    groups = [[a * NZ + b for b in range(NZ)] for a in range(NX)]
    parts = lax.all_to_all(
        summed.reshape(NZ, 32, 128), "aux", 0, 0, axis_index_groups=groups, tiled=True
    )
    return jnp.sum(parts, axis=0)


def solution(mesh):
    in_specs = (P("aux", "occ", None), P("aux", "occ", None), P("aux"), P())
    return jax.shard_map(
        per_device, mesh=mesh, in_specs=in_specs, out_specs=P("aux", "occ"), check_vma=False
    )
```

```python
import functools

import jax
import jax.numpy as jnp
from jax import lax
from jax.experimental import pallas as pl
from jax.experimental.layout import Layout, with_layout_constraint
from jax.experimental.pallas import tpu as pltpu
from jax.sharding import PartitionSpec as P

NBF = 1024
BLK = 64
NOCC = 128
AUX_DEV = 48
NX, NZ, NY, NC = 4, 8, 4, 2
CHIP_AUX = AUX_DEV // NY
CHUNKS = (6, 6)
STEPS = (2, 1, 3)
ROWS = BLK // 2
HEAD = 8
ORDER = 10**11
PAD = 8
PLACES = {
    (2, 1): ((((0, 0), (1, 0)), ((2, 0), (0, 512))), (1024 + PAD, 512 + PAD, 512)),
    (3, 0): ((((0, 0), (0, 512)), ((1, 0), (1, 512))), (1024, 1024)),
}
VMEM = pl.BlockSpec(memory_space=pltpu.VMEM)
SMEM = pl.BlockSpec(memory_space=pltpu.SMEM)
F32, BF16 = jnp.float32, jnp.bfloat16
NT = (((1,), (1,)), ((), ()))


def device_of(x, z, y, c):
    return ((x % NX) * NZ + z % NZ) * (NY * NC) + (y % NY) * NC + c % NC


def send(array, where):
    pairs = [
        (device_of(x, z, y, c), device_of(*where(x, z, y, c)))
        for x in range(NX)
        for z in range(NZ)
        for y in range(NY)
        for c in range(NC)
    ]
    return lax.ppermute(array, ("aux", "occ"), pairs)


def call(kernel, out_shape, in_specs, scratch=(), flops=0, bytes_accessed=0):
    return pl.pallas_call(
        kernel,
        out_shape=out_shape,
        in_specs=in_specs,
        out_specs=jax.tree.map(lambda _: VMEM, out_shape),
        scratch_shapes=list(scratch),
        compiler_params=pltpu.CompilerParams(vmem_limit_bytes=40 * 2**20),
        cost_estimate=pl.CostEstimate(
            flops=flops, bytes_accessed=bytes_accessed, transcendentals=0
        ),
    )


def split(values):
    high = values.astype(BF16)
    return high, (values - high.astype(F32)).astype(BF16)


def pack_kernel(pairs_ref, count_ref, tiles_ref, own, *outs):
    occ = lax.axis_index("occ")
    lane = lax.broadcasted_iota(jnp.int32, (HEAD, 128), 1)
    head = jnp.zeros((HEAD, 128), F32)
    for slot in range(2):
        live = (occ * 2 + slot < count_ref[0]).astype(jnp.int32).astype(F32)
        head = jnp.where(lane == 3 * slot + 2, live, head)
        for j in range(2):
            number = pairs_ref[0, slot : slot + 1, j : j + 1].astype(F32)
            head = jnp.where(lane == 3 * slot + j, jnp.broadcast_to(number, head.shape), head)

    def fill(out, step, start, count, headed):
        chip = lax.rem(occ // NC + step, NY)
        base = (chip * CHIP_AUX + start) * BLK
        for slot in range(2):
            out[pl.ds(slot * count * ROWS, count * ROWS), :] = tiles_ref[
                pl.ds(pl.multiple_of(base, 8) + slot, count * ROWS, stride=2), :
            ]
        if headed:
            out[pl.ds(2 * count * ROWS, HEAD), :] = head

    fill(own, 0, 0, CHIP_AUX, True)
    for j, step in enumerate(STEPS):
        fill(outs[j], step, 0, CHUNKS[0], True)
        fill(outs[3 + j], step, CHUNKS[0], CHUNKS[1], False)


def orbitals_kernel(orbitals_ref, high_ref, low_ref):
    high, low = split(orbitals_ref[...].T)
    high_ref[...] = high
    low_ref[...] = low


def picked(ref, info_ref, index):
    column = pl.multiple_of(info_ref[index, 1] * BLK, BLK)
    block = ref[pl.ds(column, BLK), :].astype(F32)
    block = jnp.where(info_ref[index, 2] > 0, block, 0.0).astype(BF16)
    zero = jnp.zeros((BLK, NOCC), BF16)
    top = jnp.concatenate([block, zero], axis=1)
    return jnp.concatenate([top, jnp.concatenate([zero, block], axis=1)], axis=0)


def half_kernel(chunk, info_ref, high_t, low_t, own, own_other, *refs):
    got, refs = refs[:3], refs[3:]
    got_other, (high_ref, low_ref, half, parts) = refs[:-4], refs[-4:]
    count, head = CHUNKS[chunk], HEAD if chunk == 0 else 0
    sources = [(ref, CHIP_AUX * ROWS, chunk * CHUNKS[0] * ROWS) for ref in (own, own_other)]
    sources += [(ref, count * ROWS, 0) for ref in got]
    if chunk == 0:
        sources += [(got_other[0], count * ROWS, j * (2 * count * ROWS + head)) for j in range(3)]
    else:
        sources += [(ref, count * ROWS, 0) for ref in got_other]
    half[...] = jnp.zeros_like(half)
    for source, (ref, stride, start) in enumerate(sources):
        for slot in range(2):
            index = source * 2 + slot
            high, low = split(ref[pl.ds(start + slot * stride, count * ROWS), :])
            weights, rest = (picked(ref, info_ref, index) for ref in (high_t, low_t))
            parts[index] = jnp.dot(
                jnp.concatenate([high, low, high], axis=1),
                jnp.concatenate([weights, weights, rest], axis=0),
                preferred_element_type=F32,
            )
    for index in range(16):
        row = pl.multiple_of(info_ref[index, 0] * BLK, BLK)
        for q in range(count):
            for odd in range(2):
                spot = pl.ds(row + odd, ROWS, stride=2)
                half[q, spot, :] += parts[
                    index, q * ROWS : (q + 1) * ROWS, odd * 128 : odd * 128 + 128
                ]
    for q in range(count):
        high, low = split(half[q])
        high_ref[:, q * 128 : (q + 1) * 128] = high
        low_ref[:, q * 128 : (q + 1) * 128] = low


def exchange_kernel(steps, parts, *refs):
    place, sizes = PLACES[steps]
    count = len(sizes)
    halves, before, outs = refs[: 2 * parts], refs[2 * parts : -count], refs[-count:]
    aux, occ = lax.axis_index("aux"), lax.axis_index("occ")
    x, y, core = aux // NZ, occ // NC, lax.rem(occ, NC)

    def rows(ref, i):
        return ref[pl.ds(pl.multiple_of(lax.rem(x + i, NX) * 256, 256), 256), :]

    def columns(ref, j):
        start = (lax.rem(y + j, NY) * NC + core) * 128
        return ref[pl.ds(pl.multiple_of(start, 128), 128), :]

    def product(row_steps, column_steps):
        high, low = (
            [jnp.concatenate([rows(ref, i) for i in row_steps], axis=0) for ref in halves[n::2]]
            for n in range(2)
        )
        col_high, col_low = (
            [jnp.concatenate([columns(ref, j) for j in column_steps], axis=0) for ref in halves[n::2]]
            for n in range(2)
        )
        return lax.dot_general(
            jnp.concatenate([*high, *high, *low], axis=1),
            jnp.concatenate([*col_high, *col_low, *col_high], axis=1),
            NT,
            preferred_element_type=F32,
        )

    def put(a, b, tile):
        which, start = place[a][b // 2]
        start += b % 2 * 256
        spot = slice(start, start + 256)
        outs[which][spot] = before[which][spot] + tile if before else tile

    @pl.when(core == 0)
    def _():
        value = product(range(NX), steps)
        for a in range(2):
            for b in range(4):
                put(a, b, value[b * 256 : (b + 1) * 256, a * 128 : (a + 1) * 128])

    @pl.when(core == 1)
    def _():
        for pair in range(2):
            value = product(steps, (2 * pair, 2 * pair + 1))
            for a in range(2):
                for b in range(2):
                    put(
                        a,
                        2 * pair + b,
                        value[a * 256 : (a + 1) * 256, b * 128 : (b + 1) * 128],
                    )

    for out in outs:
        if out.shape[0] % 512:
            out[-PAD:] = jnp.zeros((PAD, 128), F32)


def per_device(blocks, pair_list, pair_count, orbitals):
    shape = jax.ShapeDtypeStruct
    tiles = blocks.reshape(AUX_DEV, 2, ROWS, 128)
    tiles = with_layout_constraint(tiles, Layout(major_to_minor=(0, 2, 1, 3)))
    tiles = tiles.transpose(0, 2, 1, 3).reshape(AUX_DEV * BLK, 128)
    first, second = CHUNKS
    own, *packed = call(
        pack_kernel,
        [shape((2 * CHIP_AUX * ROWS + HEAD, 128), F32)]
        + [shape((2 * first * ROWS + HEAD, 128), F32)] * 3
        + [shape((2 * second * ROWS, 128), F32)] * 3,
        [VMEM, SMEM, VMEM],
    )(pair_list, pair_count, tiles)
    high_t, low_t = call(orbitals_kernel, [shape((NBF, NOCC), BF16)] * 2, [VMEM], flops=ORDER)(orbitals)

    def over_y(mine):
        return [
            send(part, lambda x, z, y, c, k=k: (x, z, y + k, c))
            for part, k in zip(mine, STEPS, strict=True)
        ]

    def over_core(part):
        return send(part, lambda x, z, y, c: (x, z, y, c + 1))

    later = over_y(packed[3:])
    got = over_y(packed[:3])
    own_other = over_core(own)
    got_other = over_core(jnp.concatenate(got))
    size = 2 * first * ROWS + HEAD
    heads = [own[2 * CHIP_AUX * ROWS], own_other[2 * CHIP_AUX * ROWS]]
    heads += [part[size - HEAD] for part in got]
    heads += [got_other[(j + 1) * size - HEAD] for j in range(3)]
    pairs = jnp.stack(heads)[:, :6].astype(jnp.int32).reshape(16, 3)

    def half(chunk, *parts):
        count = CHUNKS[chunk]
        return call(
            functools.partial(half_kernel, chunk),
            [shape((NBF, count * NOCC), BF16)] * 2,
            [SMEM] + [VMEM] * (4 + len(parts)),
            [pltpu.VMEM((count, NBF, NOCC), F32), pltpu.VMEM((16, count * ROWS, 256), F32)],
        )(pairs, high_t, low_t, own, own_other, *parts)

    def partial(steps, halves, before=()):
        return call(
            functools.partial(exchange_kernel, steps, len(halves) // 2),
            [shape((size, 128), F32) for size in PLACES[steps][1]],
            [VMEM] * (len(halves) + len(before)),
            flops=2 * 3 * 256 * 1024 * CHIP_AUX * NOCC,
        )(*halves, *before)

    halves = list(half(0, *got, got_other))
    halves[0], *later = lax.optimization_barrier((halves[0], *later))
    before = partial((2, 1), halves)
    last = half(1, *later, *(over_core(part) for part in later))
    right, left, one_a = partial((2, 1), last, before)
    three, own_part = partial((3, 0), [*halves, *last])

    def along(k, swapped):
        def where(x, z, y, c):
            return (x + k, z, y, c) if (c == 1) != swapped else (x, z, y + k, c)

        return where

    right, left = send(right, along(1, False)), send(left, along(3, False))
    three = send(jnp.concatenate([three[:512], three[512:] + left[:512]]), along(3, False))
    one_a = send(one_a + right[:512], along(1, False))
    three, one_a = lax.optimization_barrier((three, one_a))
    three += own_part
    summed = (three[:512] + one_a, three[512:] + right[512:1024])
    tiles = [tile for part in summed for tile in (part[:256], part[256:])]
    got = [send(tiles[k], along(k, True)) for k in STEPS]
    summed = tiles[0] + got[0] + got[1] + got[2]
    groups = [[a * NZ + b for b in range(NZ)] for a in range(NX)]
    parts = lax.all_to_all(
        summed.reshape(NZ, 32, 128), "aux", 0, 0, axis_index_groups=groups, tiled=True
    )
    return jnp.sum(parts, axis=0)


def solution(mesh):
    in_specs = (P("aux", "occ", None), P("aux", "occ", None), P("aux"), P())
    return jax.shard_map(
        per_device, mesh=mesh, in_specs=in_specs, out_specs=P("aux", "occ"), check_vma=False
    )
```

```python
import functools

import jax
import jax.numpy as jnp
from jax import lax
from jax.experimental import pallas as pl
from jax.experimental.layout import Layout, with_layout_constraint
from jax.experimental.pallas import tpu as pltpu
from jax.sharding import PartitionSpec as P

NBF = 1024
BLK = 64
NOCC = 128
AUX_DEV = 48
NX, NZ, NY, NC = 4, 8, 4, 2
CHIP_AUX = AUX_DEV // NY
CHUNKS = (6, 6)
STEPS = (2, 1, 3)
ROWS = BLK // 2
HEAD = 8
ORDER = 10**11
PAD = 8
VMEM = pl.BlockSpec(memory_space=pltpu.VMEM)
SMEM = pl.BlockSpec(memory_space=pltpu.SMEM)
F32, BF16 = jnp.float32, jnp.bfloat16
NT = (((1,), (1,)), ((), ()))


def device_of(x, z, y, c):
    return ((x % NX) * NZ + z % NZ) * (NY * NC) + (y % NY) * NC + c % NC


def send(array, where):
    pairs = [
        (device_of(x, z, y, c), device_of(*where(x, z, y, c)))
        for x in range(NX)
        for z in range(NZ)
        for y in range(NY)
        for c in range(NC)
    ]
    return lax.ppermute(array, ("aux", "occ"), pairs)


def call(kernel, out_shape, in_specs, scratch=(), flops=0, bytes_accessed=0):
    return pl.pallas_call(
        kernel,
        out_shape=out_shape,
        in_specs=in_specs,
        out_specs=jax.tree.map(lambda _: VMEM, out_shape),
        scratch_shapes=list(scratch),
        compiler_params=pltpu.CompilerParams(vmem_limit_bytes=40 * 2**20),
        cost_estimate=pl.CostEstimate(
            flops=flops, bytes_accessed=bytes_accessed, transcendentals=0
        ),
    )


def split(values):
    high = values.astype(BF16)
    return high, (values - high.astype(F32)).astype(BF16)


def pack_kernel(pairs_ref, count_ref, tiles_ref, own, *outs):
    occ = lax.axis_index("occ")
    lane = lax.broadcasted_iota(jnp.int32, (HEAD, 128), 1)
    head = jnp.zeros((HEAD, 128), F32)
    for slot in range(2):
        live = (occ * 2 + slot < count_ref[0]).astype(jnp.int32).astype(F32)
        head = jnp.where(lane == 3 * slot + 2, live, head)
        for j in range(2):
            number = pairs_ref[0, slot : slot + 1, j : j + 1].astype(F32)
            head = jnp.where(lane == 3 * slot + j, jnp.broadcast_to(number, head.shape), head)

    def fill(out, step, start, count, headed):
        chip = lax.rem(occ // NC + step, NY)
        base = (chip * CHIP_AUX + start) * BLK
        for slot in range(2):
            out[pl.ds(slot * count * ROWS, count * ROWS), :] = tiles_ref[
                pl.ds(pl.multiple_of(base, 8) + slot, count * ROWS, stride=2), :
            ]
        if headed:
            out[pl.ds(2 * count * ROWS, HEAD), :] = head

    fill(own, 0, 0, CHIP_AUX, True)
    for j, step in enumerate(STEPS):
        fill(outs[j], step, 0, CHUNKS[0], True)
        fill(outs[3 + j], step, CHUNKS[0], CHUNKS[1], False)


def orbitals_kernel(orbitals_ref, high_ref, low_ref):
    high, low = split(orbitals_ref[...].T)
    high_ref[...] = high
    low_ref[...] = low


def picked(ref, info_ref, index):
    column = pl.multiple_of(info_ref[index, 1] * BLK, BLK)
    block = ref[pl.ds(column, BLK), :].astype(F32)
    block = jnp.where(info_ref[index, 2] > 0, block, 0.0).astype(BF16)
    zero = jnp.zeros((BLK, NOCC), BF16)
    top = jnp.concatenate([block, zero], axis=1)
    return jnp.concatenate([top, jnp.concatenate([zero, block], axis=1)], axis=0)


def half_kernel(chunk, info_ref, high_t, low_t, own, own_other, *refs):
    got, refs = refs[:3], refs[3:]
    got_other, (high_ref, low_ref, half, parts) = refs[:-4], refs[-4:]
    count, head = CHUNKS[chunk], HEAD if chunk == 0 else 0
    sources = [(ref, CHIP_AUX * ROWS, chunk * CHUNKS[0] * ROWS) for ref in (own, own_other)]
    sources += [(ref, count * ROWS, 0) for ref in got]
    if chunk == 0:
        sources += [(got_other[0], count * ROWS, j * (2 * count * ROWS + head)) for j in range(3)]
    else:
        sources += [(ref, count * ROWS, 0) for ref in got_other]
    half[...] = jnp.zeros_like(half)
    for source, (ref, stride, start) in enumerate(sources):
        for slot in range(2):
            index = source * 2 + slot
            high, low = split(ref[pl.ds(start + slot * stride, count * ROWS), :])
            weights, rest = (picked(ref, info_ref, index) for ref in (high_t, low_t))
            parts[index] = jnp.dot(
                jnp.concatenate([high, low, high], axis=1),
                jnp.concatenate([weights, weights, rest], axis=0),
                preferred_element_type=F32,
            )
    for index in range(16):
        row = pl.multiple_of(info_ref[index, 0] * BLK, BLK)
        for q in range(count):
            for odd in range(2):
                spot = pl.ds(row + odd, ROWS, stride=2)
                half[q, spot, :] += parts[
                    index, q * ROWS : (q + 1) * ROWS, odd * 128 : odd * 128 + 128
                ]
    for q in range(count):
        high, low = split(half[q])
        high_ref[:, q * 128 : (q + 1) * 128] = high
        low_ref[:, q * 128 : (q + 1) * 128] = low


def exchange_kernel(steps, parts, *refs):
    halves, before, outs = refs[: 2 * parts], refs[2 * parts : -2], refs[-2:]
    aux, occ = lax.axis_index("aux"), lax.axis_index("occ")
    x, y, core = aux // NZ, occ // NC, lax.rem(occ, NC)

    def rows(ref, i):
        return ref[pl.ds(pl.multiple_of(lax.rem(x + i, NX) * 256, 256), 256), :]

    def columns(ref, j):
        start = (lax.rem(y + j, NY) * NC + core) * 128
        return ref[pl.ds(pl.multiple_of(start, 128), 128), :]

    def product(row_steps, column_steps):
        high, low = (
            [jnp.concatenate([rows(ref, i) for i in row_steps], axis=0) for ref in halves[n::2]]
            for n in range(2)
        )
        col_high, col_low = (
            [jnp.concatenate([columns(ref, j) for j in column_steps], axis=0) for ref in halves[n::2]]
            for n in range(2)
        )
        return lax.dot_general(
            jnp.concatenate([*high, *high, *low], axis=1),
            jnp.concatenate([*col_high, *col_low, *col_high], axis=1),
            NT,
            preferred_element_type=F32,
        )

    def put(a, b, tile):
        spot = slice(b * 256, b * 256 + 256)
        outs[a][spot] = before[a][spot] + tile if before else tile

    @pl.when(core == 0)
    def _():
        value = product(range(NX), steps)
        for a in range(2):
            for b in range(4):
                put(a, b, value[b * 256 : (b + 1) * 256, a * 128 : (a + 1) * 128])

    @pl.when(core == 1)
    def _():
        for pair in range(2):
            value = product(steps, (2 * pair, 2 * pair + 1))
            for a in range(2):
                for b in range(2):
                    put(
                        a,
                        2 * pair + b,
                        value[a * 256 : (a + 1) * 256, b * 128 : (b + 1) * 128],
                    )

    for out in outs:
        if out.shape[0] > 1024:
            out[1024:] = jnp.zeros((out.shape[0] - 1024, 128), F32)


def per_device(blocks, pair_list, pair_count, orbitals):
    shape = jax.ShapeDtypeStruct
    tiles = blocks.reshape(AUX_DEV, 2, ROWS, 128)
    tiles = with_layout_constraint(tiles, Layout(major_to_minor=(0, 2, 1, 3)))
    tiles = tiles.transpose(0, 2, 1, 3).reshape(AUX_DEV * BLK, 128)
    first, second = CHUNKS
    own, *packed = call(
        pack_kernel,
        [shape((2 * CHIP_AUX * ROWS + HEAD, 128), F32)]
        + [shape((2 * first * ROWS + HEAD, 128), F32)] * 3
        + [shape((2 * second * ROWS, 128), F32)] * 3,
        [VMEM, SMEM, VMEM],
    )(pair_list, pair_count, tiles)
    high_t, low_t = call(orbitals_kernel, [shape((NBF, NOCC), BF16)] * 2, [VMEM], flops=ORDER)(orbitals)

    def over_y(mine):
        return [
            send(part, lambda x, z, y, c, k=k: (x, z, y + k, c))
            for part, k in zip(mine, STEPS, strict=True)
        ]

    def over_core(part):
        return send(part, lambda x, z, y, c: (x, z, y, c + 1))

    later = over_y(packed[3:])
    got = over_y(packed[:3])
    own_other = over_core(own)
    got_other = over_core(jnp.concatenate(got))
    size = 2 * first * ROWS + HEAD
    heads = [own[2 * CHIP_AUX * ROWS], own_other[2 * CHIP_AUX * ROWS]]
    heads += [part[size - HEAD] for part in got]
    heads += [got_other[(j + 1) * size - HEAD] for j in range(3)]
    pairs = jnp.stack(heads)[:, :6].astype(jnp.int32).reshape(16, 3)

    def half(chunk, *parts):
        count = CHUNKS[chunk]
        return call(
            functools.partial(half_kernel, chunk),
            [shape((NBF, count * NOCC), BF16)] * 2,
            [SMEM] + [VMEM] * (4 + len(parts)),
            [pltpu.VMEM((count, NBF, NOCC), F32), pltpu.VMEM((16, count * ROWS, 256), F32)],
        )(pairs, high_t, low_t, own, own_other, *parts)

    def partial(steps, halves, before=()):
        return call(
            functools.partial(exchange_kernel, steps, len(halves) // 2),
            [shape((4 * 256 + (0 if 0 in steps else PAD), 128), F32)] * 2,
            [VMEM] * (len(halves) + len(before)),
            flops=2 * 3 * 256 * 1024 * CHIP_AUX * NOCC,
        )(*halves, *before)

    halves = list(half(0, *got, got_other))
    halves[0], *later = lax.optimization_barrier((halves[0], *later))
    before = partial((1, 3), halves)
    last = half(1, *later, *(over_core(part) for part in later))
    one, three = partial((1, 3), last, before)
    two, summed = partial((2, 0), [*halves, *last])

    def along(k, swapped):
        def where(x, z, y, c):
            return (x + k, z, y, c) if (c == 1) != swapped else (x, z, y + k, c)

        return where

    for part, k in ((one, 1), (three, 3)):
        summed += send(part, along(k, False))[:1024]
    summed += jnp.concatenate([send(part, along(2, False)) for part in (two[:512], two[512:])])
    summed = summed.reshape(4, 256, 128)
    got = [send(summed[k], along(k, True)) for k in STEPS]
    summed = summed[0] + got[0] + got[1] + got[2]
    groups = [[a * NZ + b for b in range(NZ)] for a in range(NX)]
    parts = lax.all_to_all(
        summed.reshape(NZ, 32, 128), "aux", 0, 0, axis_index_groups=groups, tiled=True
    )
    return jnp.sum(parts, axis=0)


def solution(mesh):
    in_specs = (P("aux", "occ", None), P("aux", "occ", None), P("aux"), P())
    return jax.shard_map(
        per_device, mesh=mesh, in_specs=in_specs, out_specs=P("aux", "occ"), check_vma=False
    )
```
